256 devices in a mesh: feat: 64 (over y, z, core), rep: 4 (over x).
Axes of the slice: x: 4, y: 4, z: 8, core: 2. Of those that a mesh axis runs over, the one named last changes fastest.
Arguments:
- node_feats: bfloat16 [1024, 131072], P('feat', 'rep'), may hold values from -6 to 6
- neighbour_blocks: int32 [4, 32, 8], P('rep'), may hold values from 0 to 255
- edge_weights: bfloat16 [4, 32, 8, 128, 128], P('rep'), may hold values from 0 to 0.0625
- block_weights: bfloat16 [4, 32, 128, 128], P('rep'), may hold values from 0 to 0.015625
- owners: int32 [4, 32], P('rep'), may hold values from 0 to 63, as said below
- self_weight: bfloat16 [1024, 512], P('feat'), may hold values from -0.1875 to 0.1875
- neigh_weight: bfloat16 [1024, 512], P('feat'), may hold values from -0.1875 to 0.1875
- bias_one: float32 [512], replicated, may hold values from -3 to 3
- self_out: bfloat16 [512, 128], replicated, may hold values from -0.25 to 0.25
- neigh_out: bfloat16 [512, 128], replicated, may hold values from -0.25 to 0.25
- bias_two: float32 [128], replicated, may hold values from -3 to 3
- logit_grads: bfloat16 [4, 8192, 128], P('rep', 'feat'), may hold values from -6 to 6
Outputs:
- logits: bfloat16 [4, 8192, 128], P('rep', 'feat')
- grad_self_weight: float32 [1024, 512], P('feat')
- grad_neigh_weight: float32 [1024, 512], P('feat')
- grad_bias_one: float32 [512], replicated
- grad_self_out: float32 [512, 128], replicated
- grad_neigh_out: float32 [512, 128], replicated
- grad_bias_two: float32 [128], replicated
The draws below stay inside these ranges and needn't reach their ends.
Inputs may be any that keep to these rules, and one draw needn't show every extreme that they name: Within one group the owners are distinct device indices of feat.
All inputs are finite; a program needn't handle non-finite values.
Results may differ from the reference program's by a relative error of at most 0.006.
Values may be sent and summed in bfloat16 or wider, within the bound.
No kernel may reach another device: no remote copies, remote signals or barrier semaphores. Data moves between devices by JAX's collectives and lax.ppermute only.
A program may use at most 128 MiB of HBM per device.

```python
import jax
import jax.numpy as jnp
from jax import lax

FEATS = 1024
HID = 512
OUT = 128
BLOCK = 128
NEIGH_BLOCKS = 8
NODE_BLOCKS = 256
LAYER_BLOCKS = 32
ALL_NODES = 131072
SLOT_ROWS = 8192
N_FEAT = 64
N_REP = 4


def one_group(key):
    first, second = jax.random.split(key)
    middle = jax.random.permutation(first, N_FEAT - 2) + 1
    order = jnp.concatenate([jnp.array([N_FEAT - 1, 0], jnp.int32), middle.astype(jnp.int32)])
    half = order[:N_FEAT // 2]
    return half[jax.random.permutation(second, N_FEAT // 2)]


def draw_owners(key, part):
    key = jax.random.fold_in(key, 7)
    keys = jax.random.split(key, N_REP)
    return jax.vmap(one_group)(keys).astype(jnp.int32)


def touch_ends(drawn, key, least, high):
    longest = drawn.shape.index(max(drawn.shape))
    spots = []
    for shift in (0, 1):
        where = [jax.random.randint(jax.random.fold_in(key, axis), (), 0, length) for axis, length in enumerate(drawn.shape)]
        where[longest] = (where[longest] + shift) % drawn.shape[longest]
        spots.append(tuple(where))
    return drawn.at[spots[0]].set(least).at[spots[1]].set(high)


def level_of(own_key, shape, shards, smallest, high):
    loudness, own = 1.0, jax.random.fold_in(own_key, 6)
    for dim, blocks in shards:
        steps = jnp.exp(jax.random.uniform(jax.random.fold_in(own, dim), (blocks,), jnp.float32, smallest / len(shards), high / len(shards)))
        loudness = loudness * jnp.repeat(steps, shape[dim] // blocks).reshape([-1 if axis == dim else 1 for axis in range(len(shape))])
    return loudness


def normal_values(own_key, extent, deviation, bound, cuts=(), held_as=jnp.bfloat16):
    entries = deviation * jax.random.normal(own_key, extent, jnp.float32)
    if cuts:
        entries = entries * level_of(own_key, extent, cuts, -0.22, 0.18)
    return jnp.clip(entries, -bound, bound).astype(held_as)


def setup_inputs(seed: int = 0) -> dict:
    seeds = jax.random.split(jax.random.key(seed), 13)
    node_feats = normal_values(seeds[0], (FEATS, ALL_NODES), 1.0, 6.0, ((0, 64), (1, 4)))
    neighbour_blocks = touch_ends(jax.random.randint(seeds[1], (N_REP, LAYER_BLOCKS, NEIGH_BLOCKS), 0, NODE_BLOCKS), jax.random.fold_in(seeds[1], 1), 0, NODE_BLOCKS - 1).astype(jnp.int32)
    edge_weights = jnp.clip(0.0625 * jax.random.uniform(seeds[2], (N_REP, LAYER_BLOCKS, NEIGH_BLOCKS, BLOCK, BLOCK), jnp.float32) ** level_of(seeds[2], (N_REP, LAYER_BLOCKS, NEIGH_BLOCKS, BLOCK, BLOCK), ((0, 4),), -0.2, 0.2), 0.0, 0.0625).astype(jnp.bfloat16)
    block_weights = jnp.clip(0.015625 * jax.random.uniform(seeds[3], (N_REP, LAYER_BLOCKS, BLOCK, BLOCK), jnp.float32) ** level_of(seeds[3], (N_REP, LAYER_BLOCKS, BLOCK, BLOCK), ((0, 4),), -0.2, 0.2), 0.0, 0.015625).astype(jnp.bfloat16)
    owners = draw_owners(jax.random.fold_in(seeds[12], 71), 0)
    self_weight = normal_values(seeds[5], (FEATS, HID), FEATS ** -0.5, 0.1875, ((0, 64),))
    neigh_weight = normal_values(seeds[6], (FEATS, HID), FEATS ** -0.5, 0.1875, ((0, 64),))
    bias_one = normal_values(seeds[7], (HID,), 0.5, 3.0, (), jnp.float32)
    self_out = normal_values(seeds[8], (HID, OUT), HID ** -0.5, 0.25)
    neigh_out = normal_values(seeds[9], (HID, OUT), HID ** -0.5, 0.25)
    bias_two = normal_values(seeds[10], (OUT,), 0.5, 3.0, (), jnp.float32)
    logit_grads = normal_values(seeds[11], (N_REP, SLOT_ROWS, OUT), 1.0, 6.0, ((0, 4), (1, 64)))
    return dict(node_feats=node_feats, neighbour_blocks=neighbour_blocks, edge_weights=edge_weights, block_weights=block_weights, owners=owners, self_weight=self_weight, neigh_weight=neigh_weight, bias_one=bias_one, self_out=self_out, neigh_out=neigh_out, bias_two=bias_two, logit_grads=logit_grads)


def silu_grad(value):
    sig = jax.nn.sigmoid(value)
    return sig * (1.0 + value * (1.0 - sig))

def reference(node_feats, neighbour_blocks, edge_weights, block_weights, owners, self_weight, neigh_weight, bias_one, self_out, neigh_out, bias_two, logit_grads):
    nodes = NODE_BLOCKS * BLOCK
    rows = LAYER_BLOCKS * BLOCK
    grad_s1 = jnp.zeros((FEATS, HID), jnp.float32)
    grad_n1 = jnp.zeros((FEATS, HID), jnp.float32)
    grad_b1 = jnp.zeros((HID,), jnp.float32)
    grad_s2 = jnp.zeros((HID, OUT), jnp.float32)
    grad_n2 = jnp.zeros((HID, OUT), jnp.float32)
    grad_b2 = jnp.zeros((OUT,), jnp.float32)
    outputs = []
    for group in range(N_REP):
        columns = node_feats[:, group * nodes:(group + 1) * nodes]
        spread = columns.astype(jnp.float32).reshape(FEATS, NODE_BLOCKS, BLOCK)
        picked = spread[:, neighbour_blocks[group]]
        aggregated = jnp.einsum('cbkj,bkij->bic', picked, edge_weights[group].astype(jnp.float32))
        aggregated = aggregated.reshape(rows, FEATS).astype(jnp.bfloat16)
        own_rows = columns[:, :rows].T
        pre = jnp.dot(own_rows, self_weight, preferred_element_type=jnp.float32)
        pre = pre + jnp.dot(aggregated, neigh_weight, preferred_element_type=jnp.float32) + bias_one
        hidden = jax.nn.silu(pre).astype(jnp.bfloat16)
        tiles = block_weights[group].astype(jnp.float32)
        mixed = jnp.einsum('bij,bjh->bih', tiles, hidden.reshape(LAYER_BLOCKS, BLOCK, HID).astype(jnp.float32))
        mixed = mixed.reshape(rows, HID).astype(jnp.bfloat16)
        result = jnp.dot(hidden, self_out, preferred_element_type=jnp.float32)
        result = result + jnp.dot(mixed, neigh_out, preferred_element_type=jnp.float32) + bias_two
        placed = jnp.zeros((N_FEAT, BLOCK, OUT), jnp.float32).at[owners[group]].set(result.reshape(LAYER_BLOCKS, BLOCK, OUT))
        outputs.append(placed.reshape(N_FEAT * BLOCK, OUT).astype(jnp.bfloat16))
        upstream = logit_grads[group].reshape(N_FEAT, BLOCK, OUT)[owners[group]].reshape(rows, OUT)
        grad_s2 = grad_s2 + jnp.dot(hidden.T, upstream, preferred_element_type=jnp.float32)
        grad_n2 = grad_n2 + jnp.dot(mixed.T, upstream, preferred_element_type=jnp.float32)
        grad_b2 = grad_b2 + lax.optimization_barrier(jnp.sum(upstream.astype(jnp.float32), 0))
        d_mixed = jnp.dot(upstream, neigh_out.T, preferred_element_type=jnp.float32).astype(jnp.bfloat16)
        back = jnp.einsum('bji,bjh->bih', tiles, d_mixed.reshape(LAYER_BLOCKS, BLOCK, HID).astype(jnp.float32))
        d_hidden = jnp.dot(upstream, self_out.T, preferred_element_type=jnp.float32) + back.reshape(rows, HID)
        d_pre = (d_hidden * silu_grad(pre)).astype(jnp.bfloat16)
        grad_b1 = grad_b1 + lax.optimization_barrier(jnp.sum(d_pre.astype(jnp.float32), 0))
        grad_s1 = grad_s1 + jnp.dot(own_rows.T, d_pre, preferred_element_type=jnp.float32)
        grad_n1 = grad_n1 + jnp.dot(aggregated.T, d_pre, preferred_element_type=jnp.float32)
    return (jnp.stack(outputs), grad_s1, grad_n1, grad_b1, grad_s2, grad_n2, grad_b2)
```

```python
import jax
import jax.numpy as jnp
from jax import lax
from jax.sharding import Mesh, PartitionSpec as P

Y, Z, CORES, REPS = 4, 8, 2, 4
CHIPS = Y * Z
SWAP = [(0, 1), (1, 0)]


def silu_grad(value):
    sig = jax.nn.sigmoid(value)
    return sig * (1.0 + value * (1.0 - sig))


def contract_rows(left, right):
    return lax.dot_general(
        left, right, (((0,), (0,)), ((), ())), preferred_element_type=jnp.float32
    )


def exchange(value, axes):
    return lax.all_to_all(value, axes, 0, 0, tiled=True)


def to_all(value, axes, count):
    return exchange(jnp.broadcast_to(value[None], (count,) + value.shape), axes)


def on_device(
    node_feats,
    neighbour_blocks,
    edge_weights,
    block_weights,
    owners,
    self_weight,
    neigh_weight,
    bias_one,
    self_out,
    neigh_out,
    bias_two,
    logit_grads,
):
    width = node_feats.shape[0]
    rows = block_weights.shape[-1]
    layer_blocks = owners.shape[1]
    hid, out = self_out.shape
    chips = ("y", "z")
    core = lax.axis_index("core")
    first = core == 0
    me = lax.axis_index(("y", "z", "core"))

    spread = node_feats.reshape(width, -1, rows)
    picked = spread[:, neighbour_blocks[0]]
    gathered_in = jnp.einsum(
        "cbkj,bkij->cbi", picked, edge_weights[0], preferred_element_type=jnp.float32
    ).astype(jnp.bfloat16)
    stacked = jnp.concatenate([spread[:, :layer_blocks], gathered_in], 0)
    slots = jnp.arange(Y * Z * CORES, dtype=jnp.int32).reshape(Y, Z, CORES)
    slots = slots.transpose(1, 2, 0).reshape(1, -1)
    places = (owners[0][:, None] == slots).astype(jnp.bfloat16)
    slotted = jnp.einsum(
        "cbi,bs->csi", stacked, places, preferred_element_type=jnp.float32
    ).astype(jnp.bfloat16)
    half = Y * rows
    sent = slotted.reshape(2 * width, Z, CORES * half).transpose(1, 0, 2)
    weights_one = jnp.concatenate([self_weight, neigh_weight], 0)
    weights_one = jnp.broadcast_to(weights_one[None], (Z, 2 * width, hid))
    arrived = exchange(jnp.concatenate([sent, weights_one], 2), "z")
    arrived = arrived.reshape(Z * 2 * width, CORES * half + hid)
    weights_all = arrived[:, CORES * half :]
    feats_mine = lax.dynamic_slice_in_dim(arrived, core * half, half, 1)
    feats_other = lax.dynamic_slice_in_dim(arrived, (1 - core) * half, half, 1)

    my_blocks = owners[0] == me
    filled = jnp.any(my_blocks).astype(jnp.float32)
    tile_mine = jnp.einsum(
        "bij,b->ij",
        block_weights[0],
        my_blocks.astype(jnp.bfloat16),
        preferred_element_type=jnp.float32,
    ).astype(jnp.bfloat16)
    upstream = logit_grads[0] * filled.astype(jnp.bfloat16)

    given = lax.ppermute(contract_rows(feats_other, weights_all), "core", SWAP)
    partial = (contract_rows(feats_mine, weights_all) + given).astype(jnp.bfloat16)
    partial = exchange(partial.reshape(Y, rows, hid), "y")
    pre = jnp.sum(partial.astype(jnp.float32), 0) + bias_one

    hidden = jax.nn.silu(pre).astype(jnp.bfloat16)
    mixed = jnp.dot(tile_mine, hidden, preferred_element_type=jnp.float32).astype(jnp.bfloat16)
    result = jnp.dot(hidden, self_out, preferred_element_type=jnp.float32)
    result = result + jnp.dot(mixed, neigh_out, preferred_element_type=jnp.float32) + bias_two
    out_block = (result * filled).astype(jnp.bfloat16)[None]
    d_mixed = jnp.dot(upstream, neigh_out.T, preferred_element_type=jnp.float32).astype(
        jnp.bfloat16
    )
    d_hidden = jnp.dot(upstream, self_out.T, preferred_element_type=jnp.float32) + contract_rows(
        tile_mine, d_mixed
    )
    d_pre = (d_hidden * silu_grad(pre)).astype(jnp.bfloat16)

    heads = (contract_rows(hidden, upstream), contract_rows(mixed, upstream))
    bias = jnp.concatenate(
        [jnp.sum(d_pre.astype(jnp.float32), 0), jnp.sum(upstream.astype(jnp.float32), 0)]
    ).reshape(-1, out)
    kept = jnp.concatenate([jnp.where(first, heads[0], heads[1]), bias], 0)
    given = jnp.concatenate([jnp.where(first, heads[1], heads[0]), bias], 0)
    kept = (kept + lax.ppermute(given, "core", SWAP)).astype(jnp.bfloat16)

    pad = 16
    sums = jnp.concatenate(
        [
            jnp.broadcast_to(d_pre[None], (Y, rows, hid)),
            kept[:hid].reshape(Y, hid // Y, out),
        ],
        2,
    )
    bias = jnp.pad(kept[hid:].reshape(1, -1), ((0, pad - 1), (0, 0)))
    sums = jnp.concatenate([sums, jnp.broadcast_to(bias[None], (Y, pad, hid + out))], 1)
    sums = exchange(sums, "y")
    d_mine = sums[:, :rows, :hid].reshape(half, hid)
    kept = jnp.sum(sums[:, :rows, hid:].astype(jnp.float32), 0).astype(jnp.bfloat16)
    bias = jnp.sum(sums[:, rows].astype(jnp.float32), 0).astype(jnp.bfloat16)

    d_other = lax.ppermute(d_mine, "core", SWAP)
    grads = jnp.dot(feats_mine, d_mine, preferred_element_type=jnp.float32)
    grads = grads + jnp.dot(feats_other, d_other, preferred_element_type=jnp.float32)
    grads = grads.astype(jnp.bfloat16).reshape(Z, 2 * width, hid)
    share = hid // CHIPS
    bias = bias.reshape(-1, out)
    spare = 2 * width - share
    bias = jnp.pad(bias, ((0, spare - bias.shape[0]), (0, 0)))
    extra = jnp.concatenate(
        [kept.reshape(Z, share, out), jnp.broadcast_to(bias[None], (Z, spare, out))], 1
    )
    sums = exchange(jnp.concatenate([grads, extra], 2), "z")
    sums = jnp.sum(sums.astype(jnp.float32), 0)
    sums = jnp.sum(to_all(sums, "rep", REPS), 0)
    grads = sums[:, :hid]
    bias = sums[share:, hid:].reshape(-1)

    kept = to_all(sums[:share, hid:], chips, CHIPS).reshape(hid, out)
    given = lax.ppermute(kept, "core", SWAP)
    return (
        out_block,
        grads[:width],
        grads[width:],
        bias[:hid],
        jnp.where(first, kept, given),
        jnp.where(first, given, kept),
        bias[hid : hid + out],
    )


def solution(mesh):
    fine = Mesh(mesh.devices.reshape(Y, Z, CORES, REPS), ("y", "z", "core", "rep"))
    feat = ("y", "z", "core")
    placed = (
        P(feat, "rep"),
        P("rep", None, None),
        P("rep", None, None, None, None),
        P("rep", None, None, None),
        P("rep", None),
        P(feat, None),
        P(feat, None),
        P(),
        P(),
        P(),
        P(),
        P("rep", feat, None),
    )
    return jax.shard_map(
        on_device,
        mesh=fine,
        in_specs=placed,
        out_specs=(P("rep", feat, None), P(feat, None), P(feat, None), P(), P(), P(), P()),
        check_vma=False,
    )
```

```python
import functools

import jax
import jax.numpy as jnp
from jax import lax
from jax.experimental import pallas as pl
from jax.experimental.pallas import tpu as pltpu
from jax.sharding import Mesh, PartitionSpec as P

Y, Z, CORES, REPS = 4, 8, 2, 4
CHIPS = Y * Z
SWAP = [(0, 1), (1, 0)]


def silu_grad(value):
    sig = jax.nn.sigmoid(value)
    return sig * (1.0 + value * (1.0 - sig))


def dot(left, right, left_dim, right_dim):
    return lax.dot_general(
        left, right, (((left_dim,), (right_dim,)), ((), ())), preferred_element_type=jnp.float32
    )


def exchange(value, axes):
    return lax.all_to_all(value, axes, 0, 0, tiled=True)


def to_all(value, axes, count):
    return exchange(jnp.broadcast_to(value[None], (count,) + value.shape), axes)


def swap(value):
    return lax.ppermute(value, "core", SWAP)


def shift(value, axis, count, by):
    return lax.ppermute(value, axis, [(i, (i + by) % count) for i in range(count)])


def paired(terms):
    return (terms[0] + terms[2]) + (terms[1] + terms[3])


def rep_sum(value):
    terms = [value] + [shift(value, "rep", REPS, by) for by in range(1, REPS)]
    return paired(terms)


def gather_kernel(neighbours, owners, place, feats, edges, own, near, out, *, per_step):
    step = pl.program_id(0)
    width = feats.shape[0]
    fan, rows = edges.shape[1], edges.shape[-1]
    layer_rows = Y * CORES * rows
    half = own.shape[1] // CORES

    @pl.when(step == 0)
    def _():
        out[:, :, half : half + layer_rows] = jnp.zeros((Z, 2 * width, layer_rows), out.dtype)
        for c in range(CORES):

            @pl.when(place[1] == c)
            def _(c=c):
                kept, given = c * half, (1 - c) * half
                for z in range(Z):
                    out[z, :width, :half] = own[:, kept : kept + half]
                    out[z, width:, :half] = near[:, kept : kept + half]
                    out[z, :width, half + layer_rows :] = own[:, given : given + half]
                    out[z, width:, half + layer_rows :] = near[:, given : given + half]

    for i in range(per_step):
        block = step * per_step + i
        starts = [pl.multiple_of(neighbours[block * fan + k] * rows, rows) for k in range(fan)]
        total = lax.dot_general(
            jnp.concatenate([feats[:, pl.ds(start, rows)] for start in starts], 1),
            jnp.concatenate([edges[i, k] for k in range(fan)], 1),
            (((1,), (1,)), ((), ())),
            preferred_element_type=jnp.float32,
        )
        owner = owners[block]
        core = owner & (CORES - 1)
        z = lax.shift_right_logical(owner, 1) & (Z - 1)
        y = (lax.shift_right_logical(owner, 4) - place[0]) & (Y - 1)
        lane = pl.multiple_of(half + (y * CORES + core) * rows, rows)
        out[z, :width, pl.ds(lane, rows)] = feats[:, pl.ds(pl.multiple_of(block * rows, rows), rows)]
        out[z, width:, pl.ds(lane, rows)] = total.astype(out.dtype)


def gather_rows(neighbours, owners, place, feats, edges, own, near):
    blocks, fan, rows, _ = edges.shape
    width = feats.shape[0]
    columns = Y * CORES * rows + own.shape[1]
    per_step = 8
    return pl.pallas_call(
        functools.partial(gather_kernel, per_step=per_step),
        out_shape=jax.ShapeDtypeStruct((Z, 2 * width, columns), feats.dtype),
        grid_spec=pltpu.PrefetchScalarGridSpec(
            num_scalar_prefetch=3,
            grid=(blocks // per_step,),
            in_specs=[
                pl.BlockSpec(feats.shape, lambda i, *_: (0, 0)),
                pl.BlockSpec((per_step, fan, rows, rows), lambda i, *_: (i, 0, 0, 0)),
                pl.BlockSpec(own.shape, lambda i, *_: (0, 0)),
                pl.BlockSpec(near.shape, lambda i, *_: (0, 0)),
            ],
            out_specs=pl.BlockSpec((Z, 2 * width, columns), lambda i, *_: (0, 0, 0)),
        ),
        compiler_params=pltpu.CompilerParams(vmem_limit_bytes=56 * 1024 * 1024),
        cost_estimate=pl.CostEstimate(
            flops=2 * width * blocks * fan * rows * rows,
            bytes_accessed=2 * (edges.size + feats.size),
            transcendentals=0,
        ),
        name="gather_rows",
    )(neighbours.reshape(-1), owners, place, feats, edges, own, near)


def on_device(
    node_feats,
    neighbour_blocks,
    edge_weights,
    block_weights,
    owners,
    self_weight,
    neigh_weight,
    bias_one,
    self_out,
    neigh_out,
    bias_two,
    logit_grads,
):
    width = node_feats.shape[0]
    rows = block_weights.shape[-1]
    hid, out = self_out.shape
    half = hid // 2
    chips = ("y", "z")
    core = lax.axis_index("core")
    at_y = lax.axis_index("y")
    at_z = lax.axis_index("z")
    first = core == 0

    def columns(value, which):
        return lax.dynamic_slice_in_dim(value, which * half, half, value.ndim - 1)

    span = CORES * rows
    sent = gather_rows(
        neighbour_blocks[0],
        owners[0],
        jnp.stack([at_y, core]).astype(jnp.int32),
        node_feats,
        edge_weights[0],
        self_weight,
        neigh_weight,
    )
    arrived = exchange(sent, "z").reshape(Z * 2 * width, Y * span + hid)
    from_other = swap(arrived[:, half:])
    weights_mine, feats_mine = arrived[:, :half], arrived[:, half : half + Y * span]
    weights_other, feats_other = from_other[:, Y * span :], from_other[:, : Y * span]

    my_slots = (at_y * Z + at_z) * CORES + jnp.arange(CORES, dtype=jnp.int32)
    my_blocks = owners[0][None] == my_slots[:, None]
    filled = jnp.any(my_blocks, 1)
    tiles = jnp.einsum(
        "bij,cb->cij",
        block_weights[0],
        my_blocks.astype(jnp.bfloat16),
        preferred_element_type=jnp.float32,
    ).astype(jnp.bfloat16)
    up_mine = logit_grads[0]
    up_other = swap(up_mine)
    upstream = jnp.stack(
        [jnp.where(first, up_mine, up_other), jnp.where(first, up_other, up_mine)]
    )
    upstream = upstream * filled.astype(jnp.bfloat16)[:, None, None]
    up_rows = upstream.reshape(span, out)
    self_half = lax.dynamic_slice_in_dim(self_out, core * half, half, 0)
    neigh_half = lax.dynamic_slice_in_dim(neigh_out, core * half, half, 0)
    d_mixed = dot(up_rows, neigh_half, 1, 1).astype(jnp.bfloat16).reshape(CORES, rows, half)
    d_hidden = dot(up_rows, self_half, 1, 1) + jnp.concatenate(
        [dot(tiles[i], d_mixed[i], 0, 0) for i in range(CORES)], 0
    )

    partial = dot(feats_mine, weights_mine, 0, 0) + dot(feats_other, weights_other, 0, 0)
    partial = partial.astype(jnp.bfloat16).reshape(Y, span, half)
    pre = partial[0].astype(jnp.float32)
    for by in range(1, Y):
        pre = pre + shift(partial[by], "y", Y, by).astype(jnp.float32)
    pre = pre + columns(bias_one, core)

    hidden = jax.nn.silu(pre).astype(jnp.bfloat16)
    d_pre = (d_hidden * silu_grad(pre)).astype(jnp.bfloat16)
    mixed = jnp.concatenate(
        [dot(tiles[i], hidden[i * rows : (i + 1) * rows], 1, 0) for i in range(CORES)], 0
    ).astype(jnp.bfloat16)
    result = dot(hidden, self_half, 1, 0) + dot(mixed, neigh_half, 1, 0)
    result_mine = jnp.where(first, result[:rows], result[rows:])
    result_other = jnp.where(first, result[rows:], result[:rows])
    result = result_mine + swap(result_other) + bias_two
    mine_filled = jnp.where(first, filled[0], filled[1]).astype(jnp.float32)
    out_block = (result * mine_filled).astype(jnp.bfloat16)[None]

    heads = jnp.concatenate([dot(hidden, up_rows, 0, 0), dot(mixed, up_rows, 0, 0)], 1)
    heads = heads.astype(jnp.bfloat16)
    bias = jnp.stack(
        [
            jnp.sum(d_pre.astype(jnp.float32), 0),
            jnp.pad(jnp.sum(up_rows.astype(jnp.float32), 0), (0, half - out)),
        ]
    ).astype(jnp.bfloat16)
    pad = 16
    bias = jnp.pad(bias, ((0, pad - CORES), (0, 0)))
    per_y = half // Y
    sums = []
    for by in range(Y):
        piece = lax.dynamic_slice_in_dim(heads, ((at_y - by) % Y) * per_y, per_y, 0)
        piece = jnp.concatenate([d_pre, piece, bias], 0)
        sums.append(piece if by == 0 else shift(piece, "y", Y, -by))
    extra = paired([piece[span:].astype(jnp.float32) for piece in sums]).astype(jnp.bfloat16)
    d_all = jnp.concatenate([piece[:span] for piece in sums], 0)
    grads = [
        dot(feats, d_all, 1, 0).astype(jnp.bfloat16).reshape(Z, 2 * width, half)
        for feats in (feats_mine, feats_other)
    ]
    per_z = per_y // Z
    spare = 2 * width - per_z
    heads = extra[:per_y].reshape(Z, per_z, half)
    bias = jnp.broadcast_to(extra[None, per_y : per_y + 8], (Z, 8, half))
    sums = exchange(jnp.concatenate([*grads, heads, bias], 1), "z")
    sums = jnp.sum(sums.astype(jnp.float32), 0)
    sums = jnp.sum(to_all(sums, "rep", REPS), 0)
    grads_mine, grads_other = sums[: 2 * width], sums[2 * width : 4 * width]
    heads = sums[4 * width : 4 * width + per_z]
    bias = sums[4 * width + per_z :]
    grads_other = swap(jnp.concatenate([grads_other, bias], 0))
    bias_other = grads_other[2 * width]
    grads_other = grads_other[: 2 * width]
    heads = to_all(heads, chips, CHIPS).reshape(half, 2 * out)
    heads_other = swap(heads)

    def ordered(mine, other, axis):
        return jnp.concatenate(
            [jnp.where(first, mine, other), jnp.where(first, other, mine)], axis
        )

    grads = ordered(grads_mine, grads_other, 1)
    heads = ordered(heads, heads_other, 0)
    return (
        out_block,
        grads[:width],
        grads[width:],
        ordered(bias[0], bias_other, 0),
        heads[:, :out],
        heads[:, out:],
        bias[1, :out],
    )


def solution(mesh):
    fine = Mesh(mesh.devices.reshape(Y, Z, CORES, REPS), ("y", "z", "core", "rep"))
    feat = ("y", "z", "core")
    placed = (
        P(feat, "rep"),
        P("rep", None, None),
        P("rep", None, None, None, None),
        P("rep", None, None, None),
        P("rep", None),
        P(feat, None),
        P(feat, None),
        P(),
        P(),
        P(),
        P(),
        P("rep", feat, None),
    )
    return jax.shard_map(
        on_device,
        mesh=fine,
        in_specs=placed,
        out_specs=(P("rep", feat, None), P(feat, None), P(feat, None), P(), P(), P(), P()),
        check_vma=False,
    )
```

```python
import functools

import jax
import jax.numpy as jnp
from jax import lax
from jax.experimental import pallas as pl
from jax.experimental.pallas import tpu as pltpu
from jax.sharding import Mesh, PartitionSpec as P

Y, Z, CORES, REPS = 4, 8, 2, 4
CHIPS = Y * Z
SWAP = [(0, 1), (1, 0)]


def silu_grad(value):
    sig = jax.nn.sigmoid(value)
    return sig * (1.0 + value * (1.0 - sig))


def dot(left, right, left_dim, right_dim):
    return lax.dot_general(
        left, right, (((left_dim,), (right_dim,)), ((), ())), preferred_element_type=jnp.float32
    )


def exchange(value, axes):
    return lax.all_to_all(value, axes, 0, 0, tiled=True)


def to_all(value, axes, count):
    return exchange(jnp.broadcast_to(value[None], (count,) + value.shape), axes)


def swap(value):
    return lax.ppermute(value, "core", SWAP)


def shift(value, axis, count, by):
    return lax.ppermute(value, axis, [(i, (i + by) % count) for i in range(count)])


def paired(terms):
    return (terms[0] + terms[2]) + (terms[1] + terms[3])


def rep_sum(value):
    terms = [value] + [shift(value, "rep", REPS, by) for by in range(1, REPS)]
    return paired(terms)


def gather_kernel(neighbours, owners, feats, edges, own, near, out, *, per_step):
    step = pl.program_id(0)
    width = feats.shape[0]
    fan, rows = edges.shape[1], edges.shape[-1]
    layer_rows = Y * CORES * rows
    half = own.shape[1] // CORES
    at_y, at_core = lax.axis_index("y"), lax.axis_index("core")

    @pl.when(step == 0)
    def _():
        out[:, :, half : half + layer_rows] = jnp.zeros((Z, 2 * width, layer_rows), out.dtype)
        for c in range(CORES):

            @pl.when(at_core == c)
            def _(c=c):
                kept, given = c * half, (1 - c) * half
                for z in range(Z):
                    out[z, :width, :half] = own[:, kept : kept + half]
                    out[z, width:, :half] = near[:, kept : kept + half]
                    out[z, :width, half + layer_rows :] = own[:, given : given + half]
                    out[z, width:, half + layer_rows :] = near[:, given : given + half]

    for i in range(per_step):
        block = step * per_step + i
        starts = [pl.multiple_of(neighbours[k, block] * rows, rows) for k in range(fan)]
        total = lax.dot_general(
            jnp.concatenate([feats[:, pl.ds(start, rows)] for start in starts], 1),
            jnp.concatenate([edges[i, k] for k in range(fan)], 1),
            (((1,), (1,)), ((), ())),
            preferred_element_type=jnp.float32,
        )
        owner = owners[0, block]
        core = owner & (CORES - 1)
        z = lax.shift_right_logical(owner, 1) & (Z - 1)
        y = (lax.shift_right_logical(owner, 4) - at_y) & (Y - 1)
        lane = pl.multiple_of(half + (y * CORES + core) * rows, rows)
        out[z, :width, pl.ds(lane, rows)] = feats[:, pl.ds(pl.multiple_of(block * rows, rows), rows)]
        out[z, width:, pl.ds(lane, rows)] = total.astype(out.dtype)


def gather_rows(neighbours, owners, feats, edges, own, near):
    blocks, fan, rows, _ = edges.shape
    width = feats.shape[0]
    columns = Y * CORES * rows + own.shape[1]
    per_step = 8
    return pl.pallas_call(
        functools.partial(gather_kernel, per_step=per_step),
        out_shape=jax.ShapeDtypeStruct((Z, 2 * width, columns), feats.dtype),
        grid_spec=pltpu.PrefetchScalarGridSpec(
            num_scalar_prefetch=2,
            grid=(blocks // per_step,),
            in_specs=[
                pl.BlockSpec(feats.shape, lambda i, *_: (0, 0)),
                pl.BlockSpec((per_step, fan, rows, rows), lambda i, *_: (i, 0, 0, 0)),
                pl.BlockSpec(own.shape, lambda i, *_: (0, 0)),
                pl.BlockSpec(near.shape, lambda i, *_: (0, 0)),
            ],
            out_specs=pl.BlockSpec((Z, 2 * width, columns), lambda i, *_: (0, 0, 0)),
        ),
        compiler_params=pltpu.CompilerParams(vmem_limit_bytes=56 * 1024 * 1024),
        cost_estimate=pl.CostEstimate(
            flops=2 * width * blocks * fan * rows * rows,
            bytes_accessed=2 * (edges.size + feats.size),
            transcendentals=0,
        ),
        name="gather_rows",
    )(neighbours, owners, feats, edges, own, near)


def grads_kernel(*refs):
    pieces, extras, (mine, other, out) = refs[:Y], refs[Y : 2 * Y], refs[2 * Y :]
    half = out.shape[2]
    rows = mine.shape[0] // Z
    layer_rows = mine.shape[1] - 2 * half
    d_all = jnp.concatenate([piece[...] for piece in pieces], 0)
    for i, feats in enumerate((mine[:, half : half + layer_rows], other[:, :layer_rows])):
        grads = jnp.dot(feats, d_all, preferred_element_type=jnp.float32).astype(out.dtype)
        for z in range(Z):
            out[z, i * rows : (i + 1) * rows] = grads[z * rows : (z + 1) * rows]
    extra = paired([piece[...].astype(jnp.float32) for piece in extras])
    per = half // CHIPS
    bias = extra[Z * per : Z * per + 8]
    for z in range(Z):
        block = jnp.concatenate([extra[z * per : (z + 1) * per], bias], 0)
        out[z, CORES * rows :] = block.astype(out.dtype)


def grad_parts(pieces, extras, mine, other):
    half = pieces[0].shape[1]
    rows = CORES * mine.shape[0] // Z + half // CHIPS + 8
    return pl.pallas_call(
        grads_kernel,
        out_shape=jax.ShapeDtypeStruct((Z, rows, half), pieces[0].dtype),
        compiler_params=pltpu.CompilerParams(vmem_limit_bytes=32 * 1024 * 1024),
        cost_estimate=pl.CostEstimate(
            flops=4 * mine.shape[0] * (mine.shape[1] - 2 * half) * half,
            bytes_accessed=2 * (mine.size + other.size + Y * pieces[0].size),
            transcendentals=0,
        ),
        name="grad_parts",
    )(*pieces, *extras, mine, other)


def on_device(
    node_feats,
    neighbour_blocks,
    edge_weights,
    block_weights,
    owners,
    self_weight,
    neigh_weight,
    bias_one,
    self_out,
    neigh_out,
    bias_two,
    logit_grads,
):
    width = node_feats.shape[0]
    rows = block_weights.shape[-1]
    hid, out = self_out.shape
    half = hid // 2
    chips = ("y", "z")
    core = lax.axis_index("core")
    at_y = lax.axis_index("y")
    at_z = lax.axis_index("z")
    first = core == 0

    def columns(value, which):
        return lax.dynamic_slice_in_dim(value, which * half, half, value.ndim - 1)

    span = CORES * rows
    sent = gather_rows(
        neighbour_blocks[0].T,
        owners,
        node_feats,
        edge_weights[0],
        self_weight,
        neigh_weight,
    )
    arrived = exchange(sent, "z").reshape(Z * 2 * width, Y * span + hid)
    from_other = swap(arrived[:, half:])
    weights_mine, feats_mine = arrived[:, :half], arrived[:, half : half + Y * span]
    weights_other, feats_other = from_other[:, Y * span :], from_other[:, : Y * span]

    my_slots = (at_y * Z + at_z) * CORES + jnp.arange(CORES, dtype=jnp.int32)
    my_blocks = owners[0][None] == my_slots[:, None]
    filled = jnp.any(my_blocks, 1)
    tiles = jnp.einsum(
        "bij,cb->cij",
        block_weights[0],
        my_blocks.astype(jnp.bfloat16),
        preferred_element_type=jnp.float32,
    ).astype(jnp.bfloat16)
    up_mine = logit_grads[0]
    up_other = swap(up_mine)
    upstream = jnp.stack(
        [jnp.where(first, up_mine, up_other), jnp.where(first, up_other, up_mine)]
    )
    upstream = upstream * filled.astype(jnp.bfloat16)[:, None, None]
    up_rows = upstream.reshape(span, out)
    self_half = lax.dynamic_slice_in_dim(self_out, core * half, half, 0)
    neigh_half = lax.dynamic_slice_in_dim(neigh_out, core * half, half, 0)
    d_mixed = dot(up_rows, neigh_half, 1, 1).astype(jnp.bfloat16).reshape(CORES, rows, half)
    d_hidden = dot(up_rows, self_half, 1, 1) + jnp.concatenate(
        [dot(tiles[i], d_mixed[i], 0, 0) for i in range(CORES)], 0
    )

    partial = dot(feats_mine, weights_mine, 0, 0) + dot(feats_other, weights_other, 0, 0)
    partial = partial.astype(jnp.bfloat16).reshape(Y, span, half)
    pre = partial[0].astype(jnp.float32)
    for by in range(1, Y):
        pre = pre + shift(partial[by], "y", Y, by).astype(jnp.float32)
    pre = pre + columns(bias_one, core)

    hidden = jax.nn.silu(pre).astype(jnp.bfloat16)
    d_pre = (d_hidden * silu_grad(pre)).astype(jnp.bfloat16)
    mixed = jnp.concatenate(
        [dot(tiles[i], hidden[i * rows : (i + 1) * rows], 1, 0) for i in range(CORES)], 0
    ).astype(jnp.bfloat16)
    result = dot(hidden, self_half, 1, 0) + dot(mixed, neigh_half, 1, 0)
    result_mine = jnp.where(first, result[:rows], result[rows:])
    result_other = jnp.where(first, result[rows:], result[:rows])
    result = result_mine + swap(result_other) + bias_two
    mine_filled = jnp.where(first, filled[0], filled[1]).astype(jnp.float32)
    out_block = (result * mine_filled).astype(jnp.bfloat16)[None]

    heads = jnp.concatenate([dot(hidden, up_rows, 0, 0), dot(mixed, up_rows, 0, 0)], 1)
    heads = heads.astype(jnp.bfloat16)
    bias = jnp.stack(
        [
            jnp.sum(d_pre.astype(jnp.float32), 0),
            jnp.pad(jnp.sum(up_rows.astype(jnp.float32), 0), (0, half - out)),
        ]
    ).astype(jnp.bfloat16)
    pad = 16
    bias = jnp.pad(bias, ((0, pad - CORES), (0, 0)))
    per_y = half // Y
    pieces, extras = [d_pre], []
    for by in range(1, Y):
        pieces.append(shift(d_pre, "y", Y, -by))
    for by in range(Y):
        piece = lax.dynamic_slice_in_dim(heads, ((at_y - by) % Y) * per_y, per_y, 0)
        piece = jnp.concatenate([piece, bias], 0)
        extras.append(piece if by == 0 else shift(piece, "y", Y, -by))
    per_z = per_y // Z
    sums = exchange(grad_parts(pieces, extras, arrived, from_other), "z")
    sums = jnp.sum(sums.astype(jnp.float32), 0)
    sums = rep_sum(sums)
    grads_mine, grads_other = sums[: 2 * width], sums[2 * width : 4 * width]
    heads = sums[4 * width : 4 * width + per_z]
    bias = sums[4 * width + per_z :]
    grads_other = swap(jnp.concatenate([grads_other, bias], 0))
    bias_other = grads_other[2 * width]
    grads_other = grads_other[: 2 * width]
    heads = to_all(heads, chips, CHIPS).reshape(half, 2 * out)
    heads_other = swap(heads)

    def ordered(mine, other, axis):
        return jnp.concatenate(
            [jnp.where(first, mine, other), jnp.where(first, other, mine)], axis
        )

    grads = ordered(grads_mine, grads_other, 1)
    heads = ordered(heads, heads_other, 0)
    return (
        out_block,
        grads[:width],
        grads[width:],
        ordered(bias[0], bias_other, 0),
        heads[:, :out],
        heads[:, out:],
        bias[1, :out],
    )


def solution(mesh):
    fine = Mesh(mesh.devices.reshape(Y, Z, CORES, REPS), ("y", "z", "core", "rep"))
    feat = ("y", "z", "core")
    placed = (
        P(feat, "rep"),
        P("rep", None, None),
        P("rep", None, None, None, None),
        P("rep", None, None, None),
        P("rep", None),
        P(feat, None),
        P(feat, None),
        P(),
        P(),
        P(),
        P(),
        P("rep", feat, None),
    )
    return jax.shard_map(
        on_device,
        mesh=fine,
        in_specs=placed,
        out_specs=(P("rep", feat, None), P(feat, None), P(feat, None), P(), P(), P(), P()),
        check_vma=False,
    )
```

```python
import functools

import jax
import jax.numpy as jnp
from jax import lax
from jax.experimental import pallas as pl
from jax.experimental.pallas import tpu as pltpu
from jax.sharding import Mesh, PartitionSpec as P

Y, Z, CORES, REPS = 4, 8, 2, 4
CHIPS = Y * Z
LAST_TWICE = (2, 1, 3)
SWAP = [(0, 1), (1, 0)]


def silu_grad(value):
    sig = jax.nn.sigmoid(value)
    return sig * (1.0 + value * (1.0 - sig))


def dot(left, right, left_dim, right_dim):
    return lax.dot_general(
        left, right, (((left_dim,), (right_dim,)), ((), ())), preferred_element_type=jnp.float32
    )


def exchange(value, axes):
    return lax.all_to_all(value, axes, 0, 0, tiled=True)


def to_all(value, axes, count):
    return exchange(jnp.broadcast_to(value[None], (count,) + value.shape), axes)


def swap(value):
    return lax.ppermute(value, "core", SWAP)


def shift(value, axis, count, by):
    return lax.ppermute(value, axis, [(i, (i + by) % count) for i in range(count)])


def paired(terms):
    return (terms[0] + terms[2]) + (terms[1] + terms[3])


def rep_sum(value):
    terms = {0: value}
    for by in LAST_TWICE:
        terms[by] = shift(value, "rep", REPS, by)
    return (terms[1] + terms[3]) + (terms[0] + terms[2])


def gather_kernel(neighbours, owners, feats, edges, own, near, out, *, per_step):
    step = pl.program_id(0)
    width = feats.shape[0]
    fan, rows = edges.shape[1], edges.shape[-1]
    layer_rows = Y * CORES * rows
    half = own.shape[1] // CORES
    at_y, at_core = lax.axis_index("y"), lax.axis_index("core")

    @pl.when(step == 0)
    def _():
        out[:, :, half : half + layer_rows] = jnp.zeros((Z, 2 * width, layer_rows), out.dtype)
        for c in range(CORES):

            @pl.when(at_core == c)
            def _(c=c):
                kept, given = c * half, (1 - c) * half
                for z in range(Z):
                    out[z, :width, :half] = own[:, kept : kept + half]
                    out[z, width:, :half] = near[:, kept : kept + half]
                    out[z, :width, half + layer_rows :] = own[:, given : given + half]
                    out[z, width:, half + layer_rows :] = near[:, given : given + half]

    for i in range(per_step):
        block = step * per_step + i
        starts = [pl.multiple_of(neighbours[k, block] * rows, rows) for k in range(fan)]
        total = lax.dot_general(
            jnp.concatenate([feats[:, pl.ds(start, rows)] for start in starts], 1),
            jnp.concatenate([edges[i, k] for k in range(fan)], 1),
            (((1,), (1,)), ((), ())),
            preferred_element_type=jnp.float32,
        )
        owner = owners[0, block]
        core = owner & (CORES - 1)
        z = lax.shift_right_logical(owner, 1) & (Z - 1)
        y = (lax.shift_right_logical(owner, 4) - at_y) & (Y - 1)
        lane = pl.multiple_of(half + (y * CORES + core) * rows, rows)
        out[z, :width, pl.ds(lane, rows)] = feats[:, pl.ds(pl.multiple_of(block * rows, rows), rows)]
        out[z, width:, pl.ds(lane, rows)] = total.astype(out.dtype)


def gather_rows(neighbours, owners, feats, edges, own, near):
    blocks, fan, rows, _ = edges.shape
    width = feats.shape[0]
    columns = Y * CORES * rows + own.shape[1]
    per_step = 16
    return pl.pallas_call(
        functools.partial(gather_kernel, per_step=per_step),
        out_shape=jax.ShapeDtypeStruct((Z, 2 * width, columns), feats.dtype),
        grid_spec=pltpu.PrefetchScalarGridSpec(
            num_scalar_prefetch=2,
            grid=(blocks // per_step,),
            in_specs=[
                pl.BlockSpec(feats.shape, lambda i, *_: (0, 0)),
                pl.BlockSpec((per_step, fan, rows, rows), lambda i, *_: (i, 0, 0, 0)),
                pl.BlockSpec(own.shape, lambda i, *_: (0, 0)),
                pl.BlockSpec(near.shape, lambda i, *_: (0, 0)),
            ],
            out_specs=pl.BlockSpec((Z, 2 * width, columns), lambda i, *_: (0, 0, 0)),
        ),
        compiler_params=pltpu.CompilerParams(vmem_limit_bytes=56 * 1024 * 1024),
        cost_estimate=pl.CostEstimate(
            flops=2 * width * blocks * fan * rows * rows,
            bytes_accessed=2 * (edges.size + feats.size),
            transcendentals=0,
        ),
        name="gather_rows",
    )(neighbours, owners, feats, edges, own, near)


def grads_kernel(*refs):
    pieces, extras, (mine, other, out) = refs[:Y], refs[Y : 2 * Y], refs[2 * Y :]
    half = out.shape[2]
    rows = mine.shape[0] // Z
    layer_rows = mine.shape[1] - 2 * half
    pieces = (pieces[0], pieces[2], pieces[1], pieces[3])
    d_all = jnp.concatenate([piece[...] for piece in pieces], 0)
    for i, feats in enumerate((mine[:, half : half + layer_rows], other[:, :layer_rows])):
        grads = jnp.dot(feats, d_all, preferred_element_type=jnp.float32).astype(out.dtype)
        for z in range(Z):
            out[z, i * rows : (i + 1) * rows] = grads[z * rows : (z + 1) * rows]
    extra = paired([piece[...].astype(jnp.float32) for piece in extras])
    per = half // CHIPS
    bias = extra[Z * per : Z * per + 8]
    for z in range(Z):
        block = jnp.concatenate([extra[z * per : (z + 1) * per], bias], 0)
        out[z, CORES * rows :] = block.astype(out.dtype)


def grad_parts(pieces, extras, mine, other):
    half = pieces[0].shape[1]
    rows = CORES * mine.shape[0] // Z + half // CHIPS + 8
    return pl.pallas_call(
        grads_kernel,
        out_shape=jax.ShapeDtypeStruct((Z, rows, half), pieces[0].dtype),
        compiler_params=pltpu.CompilerParams(vmem_limit_bytes=32 * 1024 * 1024),
        cost_estimate=pl.CostEstimate(
            flops=4 * mine.shape[0] * (mine.shape[1] - 2 * half) * half,
            bytes_accessed=2 * (mine.size + other.size + Y * pieces[0].size),
            transcendentals=0,
        ),
        name="grad_parts",
    )(*pieces, *extras, mine, other)


def on_device(
    node_feats,
    neighbour_blocks,
    edge_weights,
    block_weights,
    owners,
    self_weight,
    neigh_weight,
    bias_one,
    self_out,
    neigh_out,
    bias_two,
    logit_grads,
):
    width = node_feats.shape[0]
    rows = block_weights.shape[-1]
    hid, out = self_out.shape
    half = hid // 2
    chips = ("y", "z")
    core = lax.axis_index("core")
    at_y = lax.axis_index("y")
    at_z = lax.axis_index("z")
    first = core == 0

    def columns(value, which):
        return lax.dynamic_slice_in_dim(value, which * half, half, value.ndim - 1)

    span = CORES * rows
    sent = gather_rows(
        neighbour_blocks[0].T,
        owners,
        node_feats,
        edge_weights[0],
        self_weight,
        neigh_weight,
    )
    arrived = exchange(sent, "z").reshape(Z * 2 * width, Y * span + hid)
    from_other = swap(arrived[:, half:])
    weights_mine, feats_mine = arrived[:, :half], arrived[:, half : half + Y * span]
    weights_other, feats_other = from_other[:, Y * span :], from_other[:, : Y * span]

    my_slots = (at_y * Z + at_z) * CORES + jnp.arange(CORES, dtype=jnp.int32)
    my_blocks = owners[0][None] == my_slots[:, None]
    filled = jnp.any(my_blocks, 1)
    tiles = jnp.einsum(
        "bij,cb->cij",
        block_weights[0],
        my_blocks.astype(jnp.bfloat16),
        preferred_element_type=jnp.float32,
    ).astype(jnp.bfloat16)
    up_mine = logit_grads[0]
    up_other = swap(up_mine)
    upstream = jnp.stack(
        [jnp.where(first, up_mine, up_other), jnp.where(first, up_other, up_mine)]
    )
    upstream = upstream * filled.astype(jnp.bfloat16)[:, None, None]
    up_rows = upstream.reshape(span, out)
    self_half = lax.dynamic_slice_in_dim(self_out, core * half, half, 0)
    neigh_half = lax.dynamic_slice_in_dim(neigh_out, core * half, half, 0)
    d_mixed = dot(up_rows, neigh_half, 1, 1).astype(jnp.bfloat16).reshape(CORES, rows, half)
    d_hidden = dot(up_rows, self_half, 1, 1) + jnp.concatenate(
        [dot(tiles[i], d_mixed[i], 0, 0) for i in range(CORES)], 0
    )

    partial = dot(feats_mine, weights_mine, 0, 0) + dot(feats_other, weights_other, 0, 0)
    partial = partial.astype(jnp.bfloat16).reshape(Y, span, half)
    pre = partial[0].astype(jnp.float32)
    for by in LAST_TWICE:
        pre = pre + shift(partial[by], "y", Y, by).astype(jnp.float32)
    pre = pre + columns(bias_one, core)

    hidden = jax.nn.silu(pre).astype(jnp.bfloat16)
    d_pre = (d_hidden * silu_grad(pre)).astype(jnp.bfloat16)
    mixed = jnp.concatenate(
        [dot(tiles[i], hidden[i * rows : (i + 1) * rows], 1, 0) for i in range(CORES)], 0
    ).astype(jnp.bfloat16)
    result = dot(hidden, self_half, 1, 0) + dot(mixed, neigh_half, 1, 0)
    result_mine = jnp.where(first, result[:rows], result[rows:])
    result_other = jnp.where(first, result[rows:], result[:rows])
    result = result_mine + swap(result_other) + bias_two
    mine_filled = jnp.where(first, filled[0], filled[1]).astype(jnp.float32)
    out_block = (result * mine_filled).astype(jnp.bfloat16)[None]

    heads = jnp.concatenate([dot(hidden, up_rows, 0, 0), dot(mixed, up_rows, 0, 0)], 1)
    heads = heads.astype(jnp.bfloat16)
    bias = jnp.stack(
        [
            jnp.sum(d_pre.astype(jnp.float32), 0),
            jnp.pad(jnp.sum(up_rows.astype(jnp.float32), 0), (0, half - out)),
        ]
    ).astype(jnp.bfloat16)
    pad = 16
    bias = jnp.pad(bias, ((0, pad - CORES), (0, 0)))
    per_y = half // Y
    pieces, extras = [d_pre], []
    for by in LAST_TWICE:
        pieces.append(shift(d_pre, "y", Y, -by))
    for by in range(Y):
        piece = lax.dynamic_slice_in_dim(heads, ((at_y - by) % Y) * per_y, per_y, 0)
        piece = jnp.concatenate([piece, bias], 0)
        extras.append(piece if by == 0 else shift(piece, "y", Y, -by))
    per_z = per_y // Z
    sums = exchange(grad_parts(pieces, extras, arrived, from_other), "z")
    sums = jnp.sum(sums.astype(jnp.float32), 0)
    sums = rep_sum(sums)
    grads_mine, grads_other = sums[: 2 * width], sums[2 * width : 4 * width]
    heads = sums[4 * width : 4 * width + per_z]
    bias = sums[4 * width + per_z :]
    grads_other = swap(jnp.concatenate([grads_other, bias], 0))
    bias_other = grads_other[2 * width]
    grads_other = grads_other[: 2 * width]
    heads = to_all(heads, chips, CHIPS).reshape(half, 2 * out)
    heads_other = swap(heads)

    def ordered(mine, other, axis):
        return jnp.concatenate(
            [jnp.where(first, mine, other), jnp.where(first, other, mine)], axis
        )

    grads = ordered(grads_mine, grads_other, 1)
    heads = ordered(heads, heads_other, 0)
    return (
        out_block,
        grads[:width],
        grads[width:],
        ordered(bias[0], bias_other, 0),
        heads[:, :out],
        heads[:, out:],
        bias[1, :out],
    )


def solution(mesh):
    fine = Mesh(mesh.devices.reshape(Y, Z, CORES, REPS), ("y", "z", "core", "rep"))
    feat = ("y", "z", "core")
    placed = (
        P(feat, "rep"),
        P("rep", None, None),
        P("rep", None, None, None, None),
        P("rep", None, None, None),
        P("rep", None),
        P(feat, None),
        P(feat, None),
        P(),
        P(),
        P(),
        P(),
        P("rep", feat, None),
    )
    return jax.shard_map(
        on_device,
        mesh=fine,
        in_specs=placed,
        out_specs=(P("rep", feat, None), P(feat, None), P(feat, None), P(), P(), P(), P()),
        check_vma=False,
    )
```

```python
import functools

import jax
import jax.numpy as jnp
from jax import lax
from jax.experimental import pallas as pl
from jax.experimental.pallas import tpu as pltpu
from jax.sharding import Mesh, PartitionSpec as P

Y, Z, CORES, REPS = 4, 8, 2, 4
CHIPS = Y * Z
LAST_TWICE = (2, 1, 3)
SWAP = [(0, 1), (1, 0)]


def silu_grad(value):
    sig = jax.nn.sigmoid(value)
    return sig * (1.0 + value * (1.0 - sig))


def dot(left, right, left_dim, right_dim):
    return lax.dot_general(
        left, right, (((left_dim,), (right_dim,)), ((), ())), preferred_element_type=jnp.float32
    )


def exchange(value, axes):
    return lax.all_to_all(value, axes, 0, 0, tiled=True)


def to_all(value, axes, count):
    return exchange(jnp.broadcast_to(value[None], (count,) + value.shape), axes)


def swap(value):
    return lax.ppermute(value, "core", SWAP)


def shift(value, axis, count, by):
    return lax.ppermute(value, axis, [(i, (i + by) % count) for i in range(count)])


def paired(terms):
    return (terms[0] + terms[2]) + (terms[1] + terms[3])


def rep_sum(value):
    terms = {0: value}
    for by in LAST_TWICE:
        terms[by] = shift(value, "rep", REPS, by)
    return (terms[1] + terms[3]) + (terms[0] + terms[2])


def gather_kernel(neighbours, owners, feats, edges, own, near, out, *, per_step):
    step = pl.program_id(0)
    width = feats.shape[0]
    fan, rows = edges.shape[1], edges.shape[-1]
    layer_rows = Y * CORES * rows
    half = own.shape[1] // CORES
    at_y, at_core = lax.axis_index("y"), lax.axis_index("core")

    @pl.when(step == 0)
    def _():
        out[:, :, half : half + layer_rows] = jnp.zeros((Z, 2 * width, layer_rows), out.dtype)
        for c in range(CORES):

            @pl.when(at_core == c)
            def _(c=c):
                kept, given = c * half, (1 - c) * half
                for z in range(Z):
                    out[z, :width, :half] = own[:, kept : kept + half]
                    out[z, width:, :half] = near[:, kept : kept + half]
                    out[z, :width, half + layer_rows :] = own[:, given : given + half]
                    out[z, width:, half + layer_rows :] = near[:, given : given + half]

    for i in range(per_step):
        block = step * per_step + i
        starts = [pl.multiple_of(neighbours[k, block] * rows, rows) for k in range(fan)]
        total = lax.dot_general(
            jnp.concatenate([feats[:, pl.ds(start, rows)] for start in starts], 1),
            jnp.concatenate([edges[i, k] for k in range(fan)], 1),
            (((1,), (1,)), ((), ())),
            preferred_element_type=jnp.float32,
        )
        owner = owners[0, block]
        core = owner & (CORES - 1)
        z = lax.shift_right_logical(owner, 1) & (Z - 1)
        y = (lax.shift_right_logical(owner, 4) - at_y) & (Y - 1)
        lane = pl.multiple_of(half + (y * CORES + core) * rows, rows)
        out[z, :width, pl.ds(lane, rows)] = feats[:, pl.ds(pl.multiple_of(block * rows, rows), rows)]
        out[z, width:, pl.ds(lane, rows)] = total.astype(out.dtype)


def gather_rows(neighbours, owners, feats, edges, own, near):
    blocks, fan, rows, _ = edges.shape
    width = feats.shape[0]
    columns = Y * CORES * rows + own.shape[1]
    per_step = 16
    return pl.pallas_call(
        functools.partial(gather_kernel, per_step=per_step),
        out_shape=jax.ShapeDtypeStruct((Z, 2 * width, columns), feats.dtype),
        grid_spec=pltpu.PrefetchScalarGridSpec(
            num_scalar_prefetch=2,
            grid=(blocks // per_step,),
            in_specs=[
                pl.BlockSpec(feats.shape, lambda i, *_: (0, 0)),
                pl.BlockSpec((per_step, fan, rows, rows), lambda i, *_: (i, 0, 0, 0)),
                pl.BlockSpec(own.shape, lambda i, *_: (0, 0)),
                pl.BlockSpec(near.shape, lambda i, *_: (0, 0)),
            ],
            out_specs=pl.BlockSpec((Z, 2 * width, columns), lambda i, *_: (0, 0, 0)),
        ),
        compiler_params=pltpu.CompilerParams(vmem_limit_bytes=56 * 1024 * 1024),
        cost_estimate=pl.CostEstimate(
            flops=2 * width * blocks * fan * rows * rows,
            bytes_accessed=2 * (edges.size + feats.size),
            transcendentals=0,
        ),
        name="gather_rows",
    )(neighbours, owners, feats, edges, own, near)


def grads_kernel(*refs):
    pieces, extras, (bias, mine, other, out) = refs[:Y], refs[Y : 2 * Y], refs[2 * Y :]
    half = out.shape[2]
    rows = mine.shape[0] // Z
    layer_rows = mine.shape[1] - 2 * half
    pieces = (pieces[0], pieces[2], pieces[1], pieces[3])
    d_all = jnp.concatenate([piece[...] for piece in pieces], 0)
    for i, feats in enumerate((mine[:, half : half + layer_rows], other[:, :layer_rows])):
        grads = jnp.dot(feats, d_all, preferred_element_type=jnp.float32).astype(out.dtype)
        for z in range(Z):
            out[z, i * rows : (i + 1) * rows] = grads[z * rows : (z + 1) * rows]
    extra = paired([piece[...].astype(jnp.float32) for piece in extras])
    per = half // CHIPS
    first_row = lax.broadcasted_iota(jnp.int32, bias.shape, 0) == 0
    sums = paired([jnp.sum(piece[...].astype(jnp.float32), 0, keepdims=True) for piece in pieces])
    sums = jnp.where(first_row, sums, bias[...])
    for z in range(Z):
        block = jnp.concatenate([extra[z * per : (z + 1) * per], sums], 0)
        out[z, CORES * rows :] = block.astype(out.dtype)


def grad_parts(pieces, extras, bias, mine, other):
    half = pieces[0].shape[1]
    rows = CORES * mine.shape[0] // Z + half // CHIPS + 8
    return pl.pallas_call(
        grads_kernel,
        out_shape=jax.ShapeDtypeStruct((Z, rows, half), pieces[0].dtype),
        compiler_params=pltpu.CompilerParams(vmem_limit_bytes=32 * 1024 * 1024),
        cost_estimate=pl.CostEstimate(
            flops=4 * mine.shape[0] * (mine.shape[1] - 2 * half) * half,
            bytes_accessed=2 * (mine.size + other.size + Y * pieces[0].size),
            transcendentals=0,
        ),
        name="grad_parts",
    )(*pieces, *extras, bias, mine, other)


def on_device(
    node_feats,
    neighbour_blocks,
    edge_weights,
    block_weights,
    owners,
    self_weight,
    neigh_weight,
    bias_one,
    self_out,
    neigh_out,
    bias_two,
    logit_grads,
):
    width = node_feats.shape[0]
    rows = block_weights.shape[-1]
    hid, out = self_out.shape
    half = hid // 2
    chips = ("y", "z")
    core = lax.axis_index("core")
    at_y = lax.axis_index("y")
    at_z = lax.axis_index("z")
    first = core == 0

    def columns(value, which):
        return lax.dynamic_slice_in_dim(value, which * half, half, value.ndim - 1)

    span = CORES * rows
    sent = gather_rows(
        neighbour_blocks[0].T,
        owners,
        node_feats,
        edge_weights[0],
        self_weight,
        neigh_weight,
    )
    arrived = exchange(sent, "z").reshape(Z * 2 * width, Y * span + hid)
    from_other = swap(arrived[:, half:])
    weights_mine, feats_mine = arrived[:, :half], arrived[:, half : half + Y * span]
    weights_other, feats_other = from_other[:, Y * span :], from_other[:, : Y * span]

    my_slots = (at_y * Z + at_z) * CORES + jnp.arange(CORES, dtype=jnp.int32)
    my_blocks = owners[0][None] == my_slots[:, None]
    filled = jnp.any(my_blocks, 1)
    tiles = jnp.einsum(
        "bij,cb->cij",
        block_weights[0],
        my_blocks.astype(jnp.bfloat16),
        preferred_element_type=jnp.float32,
    ).astype(jnp.bfloat16)
    up_mine = logit_grads[0]
    up_other = swap(up_mine)
    upstream = jnp.stack(
        [jnp.where(first, up_mine, up_other), jnp.where(first, up_other, up_mine)]
    )
    upstream = upstream * filled.astype(jnp.bfloat16)[:, None, None]
    up_rows = upstream.reshape(span, out)
    bias = jnp.sum(up_rows.astype(jnp.float32), 0)
    bias = jnp.pad(bias[None], ((1, 6), (0, half - out)))
    bias = paired([bias] + [shift(bias, "y", Y, -by) for by in range(1, Y)])
    self_half = lax.dynamic_slice_in_dim(self_out, core * half, half, 0)
    neigh_half = lax.dynamic_slice_in_dim(neigh_out, core * half, half, 0)
    d_mixed = dot(up_rows, neigh_half, 1, 1).astype(jnp.bfloat16).reshape(CORES, rows, half)
    d_hidden = dot(up_rows, self_half, 1, 1) + jnp.concatenate(
        [dot(tiles[i], d_mixed[i], 0, 0) for i in range(CORES)], 0
    )

    partial = dot(feats_mine, weights_mine, 0, 0) + dot(feats_other, weights_other, 0, 0)
    partial = partial.astype(jnp.bfloat16).reshape(Y, span, half)
    pre = partial[0].astype(jnp.float32)
    for by in LAST_TWICE:
        pre = pre + shift(partial[by], "y", Y, by).astype(jnp.float32)
    pre = pre + columns(bias_one, core)

    hidden = jax.nn.silu(pre).astype(jnp.bfloat16)
    d_pre = (d_hidden * silu_grad(pre)).astype(jnp.bfloat16)
    mixed = jnp.concatenate(
        [dot(tiles[i], hidden[i * rows : (i + 1) * rows], 1, 0) for i in range(CORES)], 0
    ).astype(jnp.bfloat16)
    result = dot(hidden, self_half, 1, 0) + dot(mixed, neigh_half, 1, 0)
    result_mine = jnp.where(first, result[:rows], result[rows:])
    result_other = jnp.where(first, result[rows:], result[:rows])
    result = result_mine + swap(result_other) + bias_two
    mine_filled = jnp.where(first, filled[0], filled[1]).astype(jnp.float32)
    out_block = (result * mine_filled).astype(jnp.bfloat16)[None]

    heads = jnp.concatenate([dot(hidden, up_rows, 0, 0), dot(mixed, up_rows, 0, 0)], 1)
    heads = heads.astype(jnp.bfloat16)
    per_y = half // Y
    pieces, extras = [d_pre], []
    for by in LAST_TWICE:
        pieces.append(shift(d_pre, "y", Y, -by))
    for by in range(Y):
        piece = lax.dynamic_slice_in_dim(heads, ((at_y - by) % Y) * per_y, per_y, 0)
        extras.append(piece if by == 0 else shift(piece, "y", Y, -by))
    per_z = per_y // Z
    sums = exchange(grad_parts(pieces, extras, bias, arrived, from_other), "z")
    sums = jnp.sum(sums.astype(jnp.float32), 0)
    sums = rep_sum(sums)
    grads_mine, grads_other = sums[: 2 * width], sums[2 * width : 4 * width]
    heads = sums[4 * width : 4 * width + per_z]
    bias = sums[4 * width + per_z :]
    grads_other = swap(jnp.concatenate([grads_other, bias], 0))
    bias_other = grads_other[2 * width]
    grads_other = grads_other[: 2 * width]
    heads = to_all(heads, chips, CHIPS).reshape(half, 2 * out)
    heads_other = swap(heads)

    def ordered(mine, other, axis):
        return jnp.concatenate(
            [jnp.where(first, mine, other), jnp.where(first, other, mine)], axis
        )

    grads = ordered(grads_mine, grads_other, 1)
    heads = ordered(heads, heads_other, 0)
    return (
        out_block,
        grads[:width],
        grads[width:],
        ordered(bias[0], bias_other, 0),
        heads[:, :out],
        heads[:, out:],
        bias[1, :out],
    )


def solution(mesh):
    fine = Mesh(mesh.devices.reshape(Y, Z, CORES, REPS), ("y", "z", "core", "rep"))
    feat = ("y", "z", "core")
    placed = (
        P(feat, "rep"),
        P("rep", None, None),
        P("rep", None, None, None, None),
        P("rep", None, None, None),
        P("rep", None),
        P(feat, None),
        P(feat, None),
        P(),
        P(),
        P(),
        P(),
        P("rep", feat, None),
    )
    return jax.shard_map(
        on_device,
        mesh=fine,
        in_specs=placed,
        out_specs=(P("rep", feat, None), P(feat, None), P(feat, None), P(), P(), P(), P()),
        check_vma=False,
    )
```
